32 devices in a mesh: seq: 4 (over z), video: 8 (over y, x, core).
Axes of the slice: x: 2, y: 2, z: 4, core: 2. Of those that a mesh axis runs over, the one named last changes fastest.
Arguments:
- queries: bfloat16 [8, 512, 3072], P('video', 'seq'), may hold values from -256 to 256
- kv_current: bfloat16 [8, 512, 1024], P('video', 'seq'), may hold values from -6 to 6
- kv_history: bfloat16 [8, 2, 512, 1024], P('video', None, 'seq'), may hold values from -6 to 6
- noisy_latent: float32 [8, 512, 64], P('video', 'seq'), may hold values from -6 to 6
- head_weight: bfloat16 [3072, 64], replicated, may hold values from -0.109375 to 0.109375
- timesteps: int32 [8], P('video'), may hold values from 250 to 1000
- counts: int32 [8], P('video'), may hold values from 0 to 2, as said below
- past_latent: bfloat16 [8, 32, 512], P('video', 'seq'), may hold values from -6 to 6
- tile_lists: int32 [8, 32, 1], P('video', 'seq'), may hold values from 0 to 7; in each aligned block of 8 rows (0 to 7, 8 to 15, ..., all dimensions but the last counted through in order) at most 2 rows name the same one
- conv_in_weight: bfloat16 [432, 256], replicated, may hold values from -0.3125 to 0.3125
- conv_weight: bfloat16 [6912, 256], replicated, may hold values from -0.078125 to 0.078125
- norm_gain: float32 [256], replicated, may hold values from 0.1 to 1.9
Outputs:
- next_latent: bfloat16 [8, 512, 64], P('video', 'seq')
- decoded: bfloat16 [8, 64, 64, 256], P('video', 'seq')
The draws below stay inside these ranges and needn't reach their ends.
Inputs may be any that keep to these rules, and one draw needn't show every extreme that they name: `counts`: some video has 2 earlier spans and some has none. `tile_lists`: among the tiles of one device no decoder index appears more than 2 times; some device assigns exactly 2 tiles to one decoder.
All inputs are finite; a program needn't handle non-finite values.
Results may differ from the reference program's by a relative error of at most 0.006.
Values may be sent and summed in bfloat16 or wider, within the bound.
A program may use at most 128 MiB of HBM per device.

```python
import math
import jax
import jax.numpy as jnp
import numpy as np
from jax import lax

QH = 24
KVH = 4
HD = 128
LC = 16
CH = 256
HIST = 2
TPF = 4
PAST = 2
TS = 4
CAP = 2
VIDEOS = 8
SPAN = 512
TILE_DEV = 8
TILES = 32
N_SEQ = 4
N_VIDEO = 8


def shared_attention_draw(key):
    key_queries, key_rows = jax.random.split(key)
    query_values = jnp.clip(jax.random.normal(key_queries, (VIDEOS, SPAN, QH * HD), jnp.float32), -6.0, 6.0)
    row_values = jnp.clip(jax.random.normal(key_rows, (VIDEOS, SPAN, 2 * KVH * HD), jnp.float32), -6.0, 6.0)
    return (query_values, row_values)


def draw_queries(key, part):
    shared = shared_attention_draw(key)
    return shared[0].astype(jnp.bfloat16)


def draw_kv_current(key, part):
    shared = shared_attention_draw(key)
    return shared[1].astype(jnp.bfloat16)


def draw_counts(key, part):
    key = jax.random.fold_in(key, 7)
    drawn = jax.random.randint(key, (VIDEOS,), 0, HIST + 1, dtype=jnp.int32)
    first_pick = jax.random.randint(jax.random.fold_in(key, 1), (), 0, VIDEOS, dtype=jnp.int32)
    offset_pick = jax.random.randint(jax.random.fold_in(key, 2), (), 1, VIDEOS, dtype=jnp.int32)
    drawn = drawn.at[first_pick].set(HIST)
    drawn = drawn.at[(first_pick + offset_pick) % VIDEOS].set(0)
    return drawn


def plant(values, own_key, least, top_value):
    place = [jax.random.randint(jax.random.fold_in(own_key, axis), (), 0, length) for axis, length in enumerate(values.shape)]
    longest = values.shape.index(max(values.shape))
    neighbour = place[:longest] + [(place[longest] + 1) % values.shape[longest]] + place[longest + 1:]
    return values.at[tuple(place)].set(least).at[tuple(neighbour)].set(top_value)


def block_scale(stream_key, shape, shards, least, top_value):
    loudness, own = 1.0, jax.random.fold_in(stream_key, 6)
    for axis_at, parts in shards:
        steps = jnp.exp(jax.random.uniform(jax.random.fold_in(own, axis_at), (parts,), jnp.float32, least / len(shards), top_value / len(shards)))
        loudness = loudness * jnp.repeat(steps, shape[axis_at] // parts).reshape([-1 if axis == axis_at else 1 for axis in range(len(shape))])
    return loudness


def deal_out(rng, own, number, rows, count, top, most, slope):
    ranking = jax.random.permutation(rng, count)
    crowded, usual = portions_of(count, rows * top, most, slope, True), portions_of(count, rows * top, most, slope, False)
    places = jnp.arange(count)

    def named(tallies, rotation):
        used = int((tallies > 0).sum())
        fixed = max(1, used // 4)
        passed = fixed + (places - fixed + rotation * (used - fixed)) % max(1, count - fixed)
        return jnp.zeros((count,), jnp.int32).at[ranking[jnp.where(places < fixed, places, passed)]].set(jnp.asarray(tallies, jnp.int32))

    tallies = jnp.where(number % 4 == 0, named(crowded, number // 4), named(usual, number - number // 4 - 1))
    mixed = jax.random.permutation(jax.random.fold_in(own, 3), count)
    donor, taker = mixed[0:count // 2 * 2:2], mixed[1:count // 2 * 2:2]
    room = jnp.minimum(tallies[donor] - 1, most - tallies[taker]) // 2
    room = jnp.where((donor == ranking[0]) | (taker == ranking[0]) | (tallies[taker] == 0), 0, jnp.maximum(room, 0))
    passed = jax.random.randint(jax.random.fold_in(own, 4), (count // 2,), 0, 1 << 20) % (room + 1)
    tallies = tallies.at[donor].add(-passed).at[taker].add(passed)
    items = jnp.searchsorted(jnp.cumsum(tallies), jnp.arange(rows * top), side="right").astype(jnp.int32)
    listing = items.reshape(top, rows).T
    listing = listing[jax.random.permutation(jax.random.fold_in(own, 1), rows)]
    rotation = jax.random.randint(jax.random.fold_in(own, 2), (rows, 1), 0, top)
    return jnp.take_along_axis(listing, (jnp.arange(top)[None, :] + rotation) % top, axis=1)


def portions_of(amount, total, bound, slope, full):
    weights = [(1 << 20) // math.isqrt(grade ** slope) + 1 for grade in range(1, amount + 1)]
    largest = bound if full else min(bound, max(-(-total // amount), total * weights[0] // sum(weights)))
    least = 1 if total - largest >= amount - 1 else 0
    given, spare = [largest] + [least] * (amount - 1), total - largest - least * (amount - 1)
    while spare > 0:
        movable = [i for i in range(1, amount) if given[i] < largest] or [i for i in range(1, amount) if given[i] < bound]
        whole, left = sum([weights[i] for i in movable]), spare
        for i in movable:
            more = min(bound - given[i], max(1, left * weights[i] // whole), spare)
            given[i] = given[i] + more
            spare = spare - more
    return np.array(given)


def bell_draw(key, dims, width, bound, cuts=(), kind=jnp.bfloat16):
    entries = jax.random.normal(key, dims, jnp.float32) * width
    if len(cuts) > 0:
        entries = block_scale(key, dims, cuts, -0.22, 0.18) * entries
    return jnp.clip(entries, min=-bound, max=bound).astype(kind)


def setup_inputs(seed: int = 0) -> dict:
    splits = jax.random.split(jax.random.key(seed), 13)
    queries = draw_queries(jax.random.fold_in(splits[12], 71), 0)
    kv_current = draw_kv_current(jax.random.fold_in(splits[12], 71), 0)
    kv_history = bell_draw(splits[2], (VIDEOS, HIST, SPAN, 2 * KVH * HD), 1.0, 6.0, ((0, 8), (2, 4)))
    noisy_latent = bell_draw(splits[3], (VIDEOS, SPAN, 4 * LC), 1.0, 6.0, ((0, 8), (1, 4)), jnp.float32)
    head_weight = bell_draw(splits[4], (QH * HD, 4 * LC), (QH * HD) ** -0.5, 0.109375)
    timesteps = plant(jax.random.randint(splits[5], (VIDEOS,), 250, 1001), jax.random.fold_in(splits[5], 1), 250, 1000).astype(jnp.int32)
    counts = draw_counts(jax.random.fold_in(splits[12], 71), 0)
    past_latent = bell_draw(splits[7], (VIDEOS, TILES, PAST * TS * TS * LC), 1.0, 6.0, ((0, 8), (1, 4)))
    tile_lists_keys = jax.random.split(jax.random.fold_in(splits[8], 1), VIDEOS * TILES // TILE_DEV)
    tile_lists_turns = jax.random.permutation(jax.random.fold_in(splits[8], 3), VIDEOS * TILES // TILE_DEV)
    tile_lists = jax.vmap(lambda own, number: deal_out(jax.random.fold_in(splits[8], 2), own, number, TILE_DEV, N_VIDEO, 1, CAP, 2))(tile_lists_keys, tile_lists_turns).reshape((VIDEOS, TILES, 1))
    conv_in_weight = bell_draw(splits[9], (27 * LC, CH), (27 * LC) ** -0.5, 0.3125)
    conv_weight = bell_draw(splits[10], (27 * CH, CH), (27 * CH) ** -0.5, 0.078125)
    norm_gain = jnp.clip(1.0 + 0.18 * jax.random.normal(splits[11], (CH,), jnp.float32), 0.1, 1.9)
    return {"queries": queries, "kv_current": kv_current, "kv_history": kv_history, "noisy_latent": noisy_latent, "head_weight": head_weight, "timesteps": timesteps, "counts": counts, "past_latent": past_latent, "tile_lists": tile_lists, "conv_in_weight": conv_in_weight, "conv_weight": conv_weight, "norm_gain": norm_gain}


def noise_level(fraction):
    return 5.0 * fraction / (1.0 + 4.0 * fraction)

def causal_conv(field, weight, first_frame):
    frame_count = field.shape[1]
    height = field.shape[2]
    breadth = field.shape[3]
    channels = field.shape[4]
    padded = jnp.pad(field, ((0, 0), (2, 0), (1, 1), (1, 1), (0, 0)))
    pieces_list = []
    for delta_t in range(3):
        for delta_y in range(3):
            for delta_x in range(3):
                pieces_list.append(padded[:, first_frame + delta_t:frame_count + delta_t, delta_y:delta_y + height, delta_x:delta_x + breadth, :])
    stacked = jnp.concatenate(pieces_list, axis=-1)
    product = jnp.dot(stacked.reshape(-1, 27 * channels), weight, preferred_element_type=jnp.float32)
    return product.reshape(field.shape[0], frame_count - first_frame, height, breadth, weight.shape[1])

def decode_tiles(latent_tiles, conv_in_weight, conv_weight, norm_gain):
    hidden = causal_conv(latent_tiles, conv_in_weight, 0).astype(jnp.bfloat16)
    hidden = lax.optimization_barrier(hidden)
    hidden_wide = hidden.astype(jnp.float32)
    mean_square = lax.optimization_barrier(jnp.mean(hidden_wide * hidden_wide, axis=-1, keepdims=True))
    activated = jax.nn.silu(hidden_wide * lax.rsqrt(mean_square + 1e-06) * norm_gain).astype(jnp.bfloat16)
    mixed = causal_conv(activated, conv_weight, PAST)
    result = (hidden_wide[:, PAST:] + mixed).astype(jnp.bfloat16)
    return result.reshape(result.shape[0], TPF * TS * TS, result.shape[-1])

def build_tiles(latent_tokens, past_tiles):
    half_side = TS // 2
    tile_count = past_tiles.shape[0]
    shaped = latent_tokens.reshape(tile_count, TPF, half_side, half_side, 2, 2, LC)
    arranged = jnp.transpose(shaped, (0, 1, 2, 4, 3, 5, 6)).reshape(tile_count, TPF * TS * TS * LC)
    return jnp.concatenate([past_tiles, arranged], axis=-1)

def reference(queries, kv_current, kv_history, noisy_latent, head_weight, timesteps, counts, past_latent, tile_lists, conv_in_weight, conv_weight, norm_gain):
    scale = 1.0 / math.sqrt(HD)
    group_size = QH // KVH
    key_total = (HIST + 1) * SPAN

    def one_video(operands):
        video_queries, current_rows, history_rows, video_count = operands
        key_rows = jnp.concatenate([current_rows, history_rows.reshape(HIST * SPAN, 2 * KVH * HD)], axis=0)
        slot_index = jnp.arange(HIST * SPAN, dtype=jnp.int32) // SPAN
        valid = jnp.concatenate([jnp.ones((SPAN,), dtype=bool), slot_index < video_count])
        split_rows = key_rows.reshape(key_total, 2, KVH, HD)
        grouped_keys = jnp.transpose(split_rows[:, 0], (1, 0, 2))
        grouped_values = jnp.transpose(split_rows[:, 1], (1, 0, 2))
        grouped_queries = jnp.transpose(video_queries.reshape(SPAN, KVH, group_size, HD), (1, 2, 0, 3))

        def one_group(group_operands):
            query_block, key_block, value_block = group_operands
            scores = jnp.einsum('jqd,kd->jqk', query_block.astype(jnp.float32), key_block.astype(jnp.float32)) * scale
            scores = jnp.where(valid, scores, -1e+30)
            maximum = lax.optimization_barrier(jnp.max(scores, axis=-1, keepdims=True))
            weights = jnp.where(valid, jnp.exp(scores - maximum), 0.0)
            total = lax.optimization_barrier(jnp.sum(weights, axis=-1, keepdims=True))
            rounded = lax.optimization_barrier(weights.astype(jnp.bfloat16))
            return jnp.einsum('jqk,kd->jqd', rounded.astype(jnp.float32), value_block.astype(jnp.float32)) / total
        attended_groups = lax.map(one_group, (grouped_queries, grouped_keys, grouped_values))
        return jnp.transpose(attended_groups, (2, 0, 1, 3)).reshape(SPAN, QH * HD).astype(jnp.bfloat16)
    attended = lax.map(one_video, (queries, kv_current, kv_history, counts))
    velocity = jnp.dot(attended.reshape(VIDEOS * SPAN, QH * HD), head_weight, preferred_element_type=jnp.float32).reshape(VIDEOS, SPAN, 4 * LC)
    fraction = timesteps.astype(jnp.float32) / 1000.0
    step_size = noise_level(fraction - 0.25) - noise_level(fraction)
    next_latent = (noisy_latent + step_size[:, None, None] * velocity).astype(jnp.bfloat16)
    payload = build_tiles(next_latent.reshape(VIDEOS * SPAN, 4 * LC), past_latent.reshape(VIDEOS * TILES, PAST * TS * TS * LC))
    latent_tiles = payload.reshape(VIDEOS, TILES, PAST + TPF, TS, TS, LC)

    def decode_video(video_tiles):
        return decode_tiles(video_tiles, conv_in_weight, conv_weight, norm_gain)
    decoded_tiles = lax.map(decode_video, latent_tiles)
    destination = tile_lists[:, :, 0].astype(jnp.int32)
    blocks = destination.reshape(VIDEOS, N_SEQ, TILE_DEV)
    onehot = (blocks[..., None] == jnp.arange(N_VIDEO, dtype=jnp.int32)).astype(jnp.int32)
    earlier = jnp.cumsum(onehot, axis=2, dtype=jnp.int32) - onehot
    slot_rank = lax.optimization_barrier(jnp.sum(earlier * onehot, axis=-1, dtype=jnp.int32))
    seq_index = jnp.arange(N_SEQ, dtype=jnp.int32)[None, :, None]
    video_index = jnp.arange(VIDEOS, dtype=jnp.int32)[:, None, None]
    row_index = (seq_index * (N_VIDEO * CAP) + video_index * CAP + slot_rank).reshape(-1).astype(jnp.int32)
    decoded = jnp.zeros((N_VIDEO, N_SEQ * N_VIDEO * CAP, TPF * TS * TS, CH), jnp.bfloat16)
    decoded = decoded.at[destination.reshape(-1), row_index].set(decoded_tiles.reshape(VIDEOS * TILES, TPF * TS * TS, CH))
    return (next_latent, decoded)
```

```python
import functools
import math

import jax
import jax.numpy as jnp
from jax import lax
from jax.experimental import pallas as pl
from jax.experimental.pallas import tpu as pltpu
from jax.sharding import PartitionSpec as P

QH = 24
KVH = 4
HD = 128
LC = 16
CH = 256
TPF = 4
PAST = 2
TS = 4
CAP = 2
FRAMES = PAST + TPF
CELLS = TS * TS
WIDE = CELLS * LC
PACK = 16
MESH = pl.DeviceIdType.MESH
F32 = jnp.float32
BF16 = jnp.bfloat16


def noise_level(fraction):
    return 5.0 * fraction / (1.0 + 4.0 * fraction)


def iota(shape, axis):
    return lax.broadcasted_iota(jnp.int32, shape, axis)


def one_hot(condition):
    return jnp.where(condition, 1.0, 0.0).astype(BF16)


def dot(a, b):
    return jnp.dot(a, b, preferred_element_type=F32)


def step_kernel(
    n_seq,
    n_video,
    q_ref,
    kvc_ref,
    kvh_ref,
    noisy_ref,
    hw_ref,
    ts_ref,
    counts_ref,
    past_ref,
    lists_ref,
    win_ref,
    w2_ref,
    gain_ref,
    nl_ref,
    dec_ref,
    q_all,
    k_all,
    v_all,
    k_use,
    v_use,
    w_raw,
    w_low,
    w_high,
    vel_out,
    vel_in,
    win,
    w2,
    toeplitz,
    tiles_out,
    tiles_in,
    field,
    acc,
    kv_send,
    kv_recv,
    q_send,
    q_recv,
    vel_send,
    vel_recv,
    tile_send,
    tile_recv,
    own_sem,
):
    me = lax.axis_index("seq")
    mv = lax.axis_index("video")
    heads = QH // n_seq
    group = QH // KVH
    slots = kvh_ref.shape[0] + 1
    tokens = q_ref.shape[0]
    half = tokens // 2
    tile_count = tokens // (TPF * 4)
    rows = n_video * CAP

    def seq_peer(k):
        if n_seq == 4:
            return (me + 1 - 2 * (me % 2), (me + 2) % 4, 3 - me)[k - 1]
        return (me + k) % n_seq

    def video_peer(k):
        return (mv + k) % n_video

    barrier = pltpu.get_barrier_semaphore()
    for k in range(1, n_seq):
        pl.semaphore_signal(barrier, inc=1, device_id=(seq_peer(k), mv), device_id_type=MESH)
    for k in range(1, n_video):
        pl.semaphore_signal(barrier, inc=1, device_id=(me, video_peer(k)), device_id_type=MESH)
    pl.semaphore_wait(barrier, n_seq + n_video - 2)

    def kv_parts(target, owner):
        column = pl.multiple_of((target * heads // group) * HD, HD)
        key_columns = pl.ds(column, HD)
        value_columns = pl.ds(pl.multiple_of(column + KVH * HD, HD), HD)
        return (
            (kvc_ref.at[:, key_columns], k_all.at[owner, 0]),
            (kvh_ref.at[:, :, key_columns], k_all.at[owner, pl.ds(1, slots - 1)]),
            (kvc_ref.at[:, value_columns], v_all.at[owner, 0]),
            (kvh_ref.at[:, :, value_columns], v_all.at[owner, pl.ds(1, slots - 1)]),
        )

    def kv_copy(target, owner, part):
        source, place = kv_parts(target, owner)[part]
        return pltpu.make_async_remote_copy(
            source,
            place,
            kv_send.at[target, part],
            kv_recv.at[owner, part],
            device_id=(target, mv),
            device_id_type=MESH,
        )

    def q_part(target, owner, head):
        column = pl.multiple_of((target * heads + head) * HD, HD)
        return q_ref.at[:, pl.ds(column, HD)], q_all.at[owner, head]

    def q_copy(target, owner, head):
        source, place = q_part(target, owner, head)
        return pltpu.make_async_remote_copy(
            source,
            place,
            q_send.at[target, head],
            q_recv.at[owner, head],
            device_id=(target, mv),
            device_id_type=MESH,
        )

    def vel_copy(target, owner):
        return pltpu.make_async_remote_copy(
            vel_out.at[target],
            vel_in.at[owner],
            vel_send.at[target],
            vel_recv.at[owner],
            device_id=(target, mv),
            device_id_type=MESH,
        )

    def tile_copy(target, owner):
        return pltpu.make_async_remote_copy(
            tiles_out.at[target],
            tiles_in.at[owner],
            tile_send.at[target],
            tile_recv.at[owner],
            device_id=(me, target),
            device_id_type=MESH,
        )

    send_order = range(n_seq - 1, 0, -1)
    for k in send_order:
        for part in range(4):
            kv_copy(seq_peer(k), me, part).start()

    for k in send_order:
        target = seq_peer(k)

        def send_head(head, carry, target=target):
            q_copy(target, me, head).start()
            return carry

        lax.fori_loop(0, heads, send_head, 0)

    own = []
    for part, (source, place) in enumerate(kv_parts(me, me)):
        own.append(pltpu.make_async_copy(source, place, own_sem.at[part]))
    for head in range(heads):
        source, place = q_part(me, me, head)
        own.append(pltpu.make_async_copy(source, place, own_sem.at[4 + head]))
    w_rows = pl.ds(pl.multiple_of(me * heads * HD, HD), heads * HD)
    own.append(pltpu.make_async_copy(hw_ref.at[w_rows], w_raw, own_sem.at[4 + heads]))
    own.append(pltpu.make_async_copy(win_ref, win, own_sem.at[5 + heads]))
    own.append(pltpu.make_async_copy(w2_ref, w2, own_sem.at[6 + heads]))
    for copy in own:
        copy.start()

    width = w_raw.shape[1]
    own[4 + heads].wait()
    shape = (width, 2 * width)
    w_low[...] = dot(w_raw[...], one_hot(iota(shape, 1) == iota(shape, 0))).astype(BF16)
    w_high[...] = dot(w_raw[...], one_hot(iota(shape, 1) == iota(shape, 0) + width)).astype(BF16)

    def clear(cell, carry):
        toeplitz[cell] = jnp.zeros(toeplitz.shape[1:], BF16)
        return carry

    lax.fori_loop(0, CELLS, clear, 0)
    own[5 + heads].wait()
    for y in range(TS):
        for x in range(TS):
            first = max(0, x - 1)
            count = min(TS, x + 2) - first
            for yy in range(max(0, y - 1), min(TS, y + 2)):
                to = (yy * TS + first) * LC
                start = ((yy - y + 1) * 3 + first - x + 1) * LC
                toeplitz[y * TS + x, :, to : to + count * LC, :] = win[:, start : start + count * LC, :]

    token_code = jnp.zeros((1, tokens), jnp.int32)
    past_code = jnp.zeros((1, PAST * tile_count), jnp.int32)
    token_tile = iota((1, tokens), 1) // (TPF * 4)
    past_tile = iota((1, PAST * tile_count), 1) % tile_count
    for t in range(tile_count):
        code = lists_ref[t] * CAP
        for t2 in range(t):
            code = code + jnp.where(lists_ref[t2] == lists_ref[t], 1, 0)
        token_code = jnp.where(token_tile == t, code, token_code)
        past_code = jnp.where(past_tile == t, code, past_code)
    out_rows = n_video * PACK

    def row_match(columns, code, frame):
        row = iota((out_rows, columns), 0)
        place = row % PACK
        row_code = (row // PACK) * CAP + place % CAP
        return one_hot((row_code == code) & (place // CAP == frame))

    token_match = row_match(tokens, token_code, iota((1, tokens), 1) // 4 % TPF + PAST)
    past_match = row_match(
        PAST * tile_count, past_code, iota((1, PAST * tile_count), 1) // tile_count
    )
    past_wide = past_ref[...].astype(F32)
    past_rows = jnp.concatenate(
        [past_wide[:, f * WIDE : (f + 1) * WIDE] for f in range(PAST)], axis=0
    ).astype(BF16)
    past_sent = dot(past_match, past_rows)

    shape = (2 * width, WIDE)
    lane = iota(shape, 1)
    cell = lane // LC
    wanted = (cell // TS % 2 * 2 + cell % 2) * LC + lane % LC
    spread_low = one_hot(iota(shape, 0) == wanted)
    spread_high = one_hot(iota(shape, 0) == wanted + width)
    shape = (tokens, WIDE)
    cell = iota(shape, 1) // LC
    in_place = iota(shape, 0) % 4 == cell // TS // 2 * 2 + cell % TS // 2

    noisy = noisy_ref[...]
    noisy = jnp.concatenate([noisy[:half], noisy[half:]], axis=1)
    fraction = jnp.full((half, 2 * width), ts_ref[0], jnp.int32).astype(F32) / 1000.0
    step_size = noise_level(fraction - 0.25) - noise_level(fraction)

    held = jnp.full((tokens, HD), counts_ref[0], jnp.int32)

    def take_rows(source):
        key_rows = k_all[source, 0]
        k_use[source, 0] = key_rows
        v_use[source, 0, :, :HD] = v_all[source, 0]
        v_use[source, 0, :, HD:] = jnp.ones((tokens, HD), BF16)
        for slot in range(1, slots):
            valid = held >= slot
            k_use[source, slot] = jnp.where(
                valid, k_all[source, slot].astype(F32), key_rows.astype(F32)
            ).astype(BF16)
            v_use[source, slot, :, :HD] = jnp.where(
                valid, v_all[source, slot].astype(F32), 0.0
            ).astype(BF16)
            v_use[source, slot, :, HD:] = jnp.where(valid, 1.0, 0.0).astype(BF16)

    for part in range(4):
        own[part].wait()
    take_rows(me)
    for k in range(1, n_seq):
        source = seq_peer(k)
        for part in range(4):
            kv_copy(me, source, part).wait_recv()
        take_rows(source)

    scale = math.log2(math.e) / math.sqrt(HD)
    key_count = n_seq * slots * tokens

    def attend(source, head):
        keys = k_use[...].reshape(key_count, HD)
        scores = lax.dot_general(
            q_all[source, head], keys, (((1,), (1,)), ((), ())), preferred_element_type=F32
        )
        top = jnp.max(scores, axis=-1, keepdims=True)
        weights = jnp.exp2((scores - top) * scale).astype(BF16)
        mixed = dot(weights, v_use[...].reshape(key_count, 2 * HD))
        attended = (mixed[:, :HD] / mixed[:, HD:]).astype(BF16)
        columns = pl.ds(pl.multiple_of(head * HD, HD), HD)
        return dot(attended[:half], w_low[columns]) + dot(attended[half:], w_high[columns])

    for head in range(heads):
        own[4 + head].wait()
    zero = jnp.zeros((half, 2 * width), F32)
    vel_in[me] = lax.fori_loop(0, heads, lambda h, total: total + attend(me, h), zero)
    for k in range(1, n_seq):
        source = seq_peer(k)

        def one_head(head, total, source=source):
            q_copy(me, source, head).wait_recv()
            return total + attend(source, head)

        vel_out[source] = lax.fori_loop(0, heads, one_head, zero)
        vel_copy(source, me).start()

    for k in range(1, n_seq):
        vel_copy(me, seq_peer(k)).wait_recv()
    velocity = vel_in[0]
    for k in range(1, n_seq):
        velocity = velocity + vel_in[k]
    latent = (noisy + step_size * velocity).astype(BF16)

    spread = jnp.concatenate([dot(latent, spread_low), dot(latent, spread_high)], axis=0)
    spread = jnp.where(in_place, spread, 0.0).astype(BF16)
    tiles_out[...] = (
        (dot(token_match, spread) + past_sent).astype(BF16).reshape(n_video, PACK, WIDE)
    )
    for k in range(1, n_video):
        tile_copy(video_peer(k), mv).start()
    tiles_in[mv] = tiles_out[mv]
    nl_ref[:half] = latent[:, :width]
    nl_ref[half:] = latent[:, width:]

    shape = ((PAST + FRAMES) * rows, n_video * PACK)
    row = iota(shape, 0)
    item = row % rows
    frame = row // rows - PAST
    gather = one_hot(
        (iota(shape, 1) == item // CAP * PACK + frame * CAP + item % CAP) & (frame >= 0)
    )
    own[6 + heads].wait()
    for k in range(1, n_video):
        tile_copy(mv, video_peer(k)).wait_recv()
    frames = dot(gather, tiles_in[...].reshape(n_video * PACK, WIDE)).astype(BF16)
    taps = jnp.concatenate(
        [frames[dt * rows : (dt + FRAMES) * rows] for dt in range(3)], axis=1
    )

    def first_conv(cell, carry):
        hidden = dot(taps, toeplitz[cell].reshape(3 * WIDE, CH)).astype(BF16)
        wide = hidden.astype(F32)
        mean_square = jnp.mean(wide * wide, axis=-1, keepdims=True)
        unit = wide * lax.rsqrt(mean_square + 1e-06) * gain_ref[...]
        active = unit / (1.0 + jnp.exp(-unit))
        y, x = cell // TS, cell % TS
        field[y, x] = active.astype(BF16).reshape(FRAMES, rows, CH)
        acc[y, x] = wide[PAST * rows :].reshape(TPF, rows, CH)
        return carry

    lax.fori_loop(0, CELLS, first_conv, 0)

    for dy in range(3):
        for dx in range(3):
            y0, x0 = max(0, 1 - dy), max(0, 1 - dx)
            ny, nx = TS - abs(dy - 1), TS - abs(dx - 1)
            ys, xs = y0 + dy - 1, x0 + dx - 1
            lhs = jnp.concatenate(
                [
                    field[ys : ys + ny, xs : xs + nx, dt : dt + TPF].reshape(
                        ny * nx * TPF * rows, CH
                    )
                    for dt in range(3)
                ],
                axis=1,
            )
            product = dot(lhs, w2[:, dy * 3 + dx].reshape(3 * CH, CH))
            acc[y0 : y0 + ny, x0 : x0 + nx] += product.reshape(ny, nx, TPF, rows, CH)
    dec_ref[...] = acc[...].reshape(CELLS, TPF, rows, CH).astype(BF16)

    for k in range(1, n_seq):
        target = seq_peer(k)
        for part in range(4):
            kv_copy(target, me, part).wait_send()

        def sent_head(head, carry, target=target):
            q_copy(target, me, head).wait_send()
            return carry

        lax.fori_loop(0, heads, sent_head, 0)
        vel_copy(target, me).wait_send()
    for k in range(1, n_video):
        tile_copy(video_peer(k), mv).wait_send()


def on_device(
    n_seq,
    n_video,
    queries,
    kv_current,
    kv_history,
    noisy_latent,
    head_weight,
    timesteps,
    counts,
    past_latent,
    tile_lists,
    conv_in_weight,
    conv_weight,
    norm_gain,
):
    tokens = queries.shape[1]
    heads = QH // n_seq
    slots = kv_history.shape[1] + 1
    width = head_weight.shape[1]
    rows = n_video * CAP
    anywhere = pl.BlockSpec(memory_space=pl.ANY)
    vmem = pl.BlockSpec(memory_space=pltpu.VMEM)
    smem = pl.BlockSpec(memory_space=pltpu.SMEM)
    dma = pltpu.SemaphoreType.DMA
    next_latent, decoded = pl.pallas_call(
        functools.partial(step_kernel, n_seq, n_video),
        out_shape=(
            jax.ShapeDtypeStruct((tokens, width), BF16),
            jax.ShapeDtypeStruct((CELLS, TPF, rows, CH), BF16),
        ),
        in_specs=[
            anywhere,
            anywhere,
            anywhere,
            vmem,
            anywhere,
            smem,
            smem,
            vmem,
            smem,
            anywhere,
            anywhere,
            vmem,
        ],
        out_specs=(vmem, vmem),
        scratch_shapes=[
            pltpu.VMEM((n_seq, heads, tokens, HD), BF16),
            pltpu.VMEM((n_seq, slots, tokens, HD), BF16),
            pltpu.VMEM((n_seq, slots, tokens, HD), BF16),
            pltpu.VMEM((n_seq, slots, tokens, HD), BF16),
            pltpu.VMEM((n_seq, slots, tokens, 2 * HD), BF16),
            pltpu.VMEM((heads * HD, width), BF16),
            pltpu.VMEM((heads * HD, 2 * width), BF16),
            pltpu.VMEM((heads * HD, 2 * width), BF16),
            pltpu.VMEM((n_seq, tokens // 2, 2 * width), F32),
            pltpu.VMEM((n_seq, tokens // 2, 2 * width), F32),
            pltpu.VMEM((3, 9 * LC, CH), BF16),
            pltpu.VMEM((3, 9, CH, CH), BF16),
            pltpu.VMEM((CELLS, 3, WIDE, CH), BF16),
            pltpu.VMEM((n_video, PACK, WIDE), BF16),
            pltpu.VMEM((n_video, PACK, WIDE), BF16),
            pltpu.VMEM((TS, TS, FRAMES, rows, CH), BF16),
            pltpu.VMEM((TS, TS, TPF, rows, CH), F32),
            dma((n_seq, 4)),
            dma((n_seq, 4)),
            dma((n_seq, heads)),
            dma((n_seq, heads)),
            dma((n_seq,)),
            dma((n_seq,)),
            dma((n_video,)),
            dma((n_video,)),
            dma((7 + heads,)),
        ],
        compiler_params=pltpu.CompilerParams(
            collective_id=0, has_side_effects=True, vmem_limit_bytes=56 * 1024 * 1024
        ),
    )(
        queries[0],
        kv_current[0],
        kv_history[0],
        noisy_latent[0],
        head_weight,
        timesteps,
        counts,
        past_latent[0],
        tile_lists.reshape(-1),
        conv_in_weight.reshape(3, 9 * LC, CH),
        conv_weight.reshape(3, 9, CH, CH),
        norm_gain[None],
    )
    decoded = jnp.transpose(decoded, (2, 1, 0, 3)).reshape(1, rows, TPF * CELLS, CH)
    return next_latent[None], decoded


def solution(mesh):
    return jax.shard_map(
        functools.partial(on_device, mesh.shape["seq"], mesh.shape["video"]),
        mesh=mesh,
        in_specs=(
            P("video", "seq", None),
            P("video", "seq", None),
            P("video", None, "seq", None),
            P("video", "seq", None),
            P(),
            P("video"),
            P("video"),
            P("video", "seq", None),
            P("video", "seq", None),
            P(),
            P(),
            P(),
        ),
        out_specs=(P("video", "seq", None), P("video", "seq", None, None)),
        check_vma=False,
    )
```

```python
import functools
import math

import jax
import jax.numpy as jnp
from jax import lax
from jax.experimental import pallas as pl
from jax.experimental.pallas import tpu as pltpu
from jax.sharding import PartitionSpec as P

QH = 24
KVH = 4
HD = 128
LC = 16
CH = 256
TPF = 4
PAST = 2
TS = 4
CAP = 2
FRAMES = PAST + TPF
CELLS = TS * TS
WIDE = CELLS * LC
PACK = 16
MESH = pl.DeviceIdType.MESH
F32 = jnp.float32
BF16 = jnp.bfloat16


def noise_level(fraction):
    return 5.0 * fraction / (1.0 + 4.0 * fraction)


def iota(shape, axis):
    return lax.broadcasted_iota(jnp.int32, shape, axis)


def one_hot(condition):
    return jnp.where(condition, 1.0, 0.0).astype(BF16)


def dot(a, b):
    return jnp.dot(a, b, preferred_element_type=F32)


def step_kernel(
    n_seq,
    n_video,
    q_ref,
    kvc_ref,
    kvh_ref,
    noisy_ref,
    hw_ref,
    ts_ref,
    counts_ref,
    past_ref,
    lists_ref,
    win_ref,
    w2_ref,
    gain_ref,
    nl_ref,
    dec_ref,
    q_all,
    k_all,
    v_all,
    k_use,
    v_use,
    w_use,
    vel_out,
    vel_in,
    win,
    w2,
    toeplitz,
    tiles_out,
    tiles_in,
    field,
    acc,
    kv_send,
    kv_recv,
    q_send,
    q_recv,
    vel_send,
    vel_recv,
    tile_send,
    tile_recv,
    own_sem,
):
    me = lax.axis_index("seq")
    mv = lax.axis_index("video")
    heads = QH // n_seq
    group = QH // KVH
    slots = kvh_ref.shape[0] + 1
    tokens = q_ref.shape[0]
    tile_count = tokens // (TPF * 4)
    rows = n_video * CAP

    def seq_peer(k):
        if n_seq == 4:
            return (me + 1 - 2 * (me % 2), (me + 2) % 4, 3 - me)[k - 1]
        return (me + k) % n_seq

    def video_peer(k):
        return (mv + k) % n_video

    barrier = pltpu.get_barrier_semaphore()
    for k in range(1, n_seq):
        pl.semaphore_signal(barrier, inc=1, device_id=(seq_peer(k), mv), device_id_type=MESH)
    for k in range(1, n_video):
        pl.semaphore_signal(barrier, inc=1, device_id=(me, video_peer(k)), device_id_type=MESH)
    pl.semaphore_wait(barrier, n_seq + n_video - 2)

    def kv_parts(target, owner):
        column = pl.multiple_of((target * heads // group) * HD, HD)
        key_columns = pl.ds(column, HD)
        value_columns = pl.ds(pl.multiple_of(column + KVH * HD, HD), HD)
        return (
            (kvc_ref.at[:, key_columns], k_all.at[owner, 0]),
            (kvh_ref.at[:, :, key_columns], k_all.at[owner, pl.ds(1, slots - 1)]),
            (kvc_ref.at[:, value_columns], v_all.at[owner, 0]),
            (kvh_ref.at[:, :, value_columns], v_all.at[owner, pl.ds(1, slots - 1)]),
        )

    def kv_copy(target, owner, part):
        source, place = kv_parts(target, owner)[part]
        return pltpu.make_async_remote_copy(
            source,
            place,
            kv_send.at[target, part],
            kv_recv.at[owner, part],
            device_id=(target, mv),
            device_id_type=MESH,
        )

    def q_part(target, owner, head):
        column = pl.multiple_of((target * heads + head) * HD, HD)
        return q_ref.at[:, pl.ds(column, HD)], q_all.at[owner, head]

    def q_copy(target, owner, head):
        source, place = q_part(target, owner, head)
        return pltpu.make_async_remote_copy(
            source,
            place,
            q_send.at[target, head],
            q_recv.at[owner, head],
            device_id=(target, mv),
            device_id_type=MESH,
        )

    def vel_copy(target, owner):
        return pltpu.make_async_remote_copy(
            vel_out.at[target],
            vel_in.at[owner],
            vel_send.at[target],
            vel_recv.at[owner],
            device_id=(target, mv),
            device_id_type=MESH,
        )

    def tile_copy(target, owner):
        return pltpu.make_async_remote_copy(
            tiles_out.at[target],
            tiles_in.at[owner],
            tile_send.at[target],
            tile_recv.at[owner],
            device_id=(me, target),
            device_id_type=MESH,
        )

    send_order = range(n_seq - 1, 0, -1)
    for k in send_order:
        for part in range(4):
            kv_copy(seq_peer(k), me, part).start()

    for k in send_order:
        target = seq_peer(k)

        def send_head(head, carry, target=target):
            q_copy(target, me, head).start()
            return carry

        lax.fori_loop(0, heads, send_head, 0)

    own = []
    for part, (source, place) in enumerate(kv_parts(me, me)):
        own.append(pltpu.make_async_copy(source, place, own_sem.at[part]))
    for head in range(heads):
        source, place = q_part(me, me, head)
        own.append(pltpu.make_async_copy(source, place, own_sem.at[4 + head]))
    own.append(pltpu.make_async_copy(win_ref, win, own_sem.at[4 + heads]))
    own.append(pltpu.make_async_copy(w2_ref, w2, own_sem.at[5 + heads]))
    for head in range(heads):
        columns = pl.ds(pl.multiple_of((me * heads + head) * HD, HD), HD)
        own.append(
            pltpu.make_async_copy(hw_ref.at[:, columns], w_use.at[head], own_sem.at[6 + heads + head])
        )
    for copy in own:
        copy.start()

    def clear(cell, carry):
        toeplitz[cell] = jnp.zeros(toeplitz.shape[1:], BF16)
        return carry

    lax.fori_loop(0, CELLS, clear, 0)
    own[4 + heads].wait()
    for y in range(TS):
        for x in range(TS):
            first = max(0, x - 1)
            count = min(TS, x + 2) - first
            for yy in range(max(0, y - 1), min(TS, y + 2)):
                to = (yy * TS + first) * LC
                start = ((yy - y + 1) * 3 + first - x + 1) * LC
                toeplitz[y * TS + x, :, to : to + count * LC, :] = win[:, start : start + count * LC, :]

    token_code = jnp.zeros((1, tokens), jnp.int32)
    past_code = jnp.zeros((1, PAST * tile_count), jnp.int32)
    token_tile = iota((1, tokens), 1) // (TPF * 4)
    past_tile = iota((1, PAST * tile_count), 1) % tile_count
    for t in range(tile_count):
        code = lists_ref[t] * CAP
        for t2 in range(t):
            code = code + jnp.where(lists_ref[t2] == lists_ref[t], 1, 0)
        token_code = jnp.where(token_tile == t, code, token_code)
        past_code = jnp.where(past_tile == t, code, past_code)
    out_rows = n_video * PACK

    def row_match(columns, code, frame):
        row = iota((out_rows, columns), 0)
        place = row % PACK
        row_code = (row // PACK) * CAP + place % CAP
        return one_hot((row_code == code) & (place // CAP == frame))

    token_match = row_match(tokens, token_code, iota((1, tokens), 1) // 4 % TPF + PAST)
    past_match = row_match(
        PAST * tile_count, past_code, iota((1, PAST * tile_count), 1) // tile_count
    )
    past_wide = past_ref[...].astype(F32)
    past_rows = jnp.concatenate(
        [past_wide[:, f * WIDE : (f + 1) * WIDE] for f in range(PAST)], axis=0
    ).astype(BF16)
    past_sent = dot(past_match, past_rows)

    width = hw_ref.shape[0]
    shape = (width, WIDE)
    lane = iota(shape, 1)
    cell = lane // LC
    spread_lanes = one_hot(iota(shape, 0) == (cell // TS % 2 * 2 + cell % 2) * LC + lane % LC)
    shape = (tokens, WIDE)
    cell = iota(shape, 1) // LC
    in_place = iota(shape, 0) % 4 == cell // TS // 2 * 2 + cell % TS // 2

    fraction = jnp.full((width, tokens), ts_ref[0], jnp.int32).astype(F32) / 1000.0
    step_size = noise_level(fraction - 0.25) - noise_level(fraction)

    held = jnp.full((tokens, HD), counts_ref[0], jnp.int32)

    def take_rows(source):
        key_rows = k_all[source, 0]
        k_use[source, 0] = key_rows
        v_use[source, 0, :, :HD] = v_all[source, 0]
        v_use[source, 0, :, HD:] = jnp.ones((tokens, HD), BF16)
        for slot in range(1, slots):
            valid = held >= slot
            k_use[source, slot] = jnp.where(
                valid, k_all[source, slot].astype(F32), key_rows.astype(F32)
            ).astype(BF16)
            v_use[source, slot, :, :HD] = jnp.where(
                valid, v_all[source, slot].astype(F32), 0.0
            ).astype(BF16)
            v_use[source, slot, :, HD:] = jnp.where(valid, 1.0, 0.0).astype(BF16)

    for part in range(4):
        own[part].wait()
    take_rows(me)
    for k in range(1, n_seq):
        source = seq_peer(k)
        for part in range(4):
            kv_copy(me, source, part).wait_recv()
        take_rows(source)

    scale = math.log2(math.e) / math.sqrt(HD)
    key_count = n_seq * slots * tokens

    def attend(source, head):
        keys = k_use[...].reshape(key_count, HD)
        scores = lax.dot_general(
            q_all[source, head], keys, (((1,), (1,)), ((), ())), preferred_element_type=F32
        )
        top = jnp.max(scores, axis=-1, keepdims=True)
        weights = jnp.exp2((scores - top) * scale).astype(BF16)
        mixed = dot(weights, v_use[...].reshape(key_count, 2 * HD))
        attended = (mixed[:, :HD] / mixed[:, HD:]).astype(BF16)
        return lax.dot_general(
            w_use[head], attended, (((1,), (1,)), ((), ())), preferred_element_type=F32
        )

    for head in range(heads):
        own[4 + head].wait()
        own[6 + heads + head].wait()
    zero = jnp.zeros((width, tokens), F32)
    vel_in[me] = lax.fori_loop(0, heads, lambda h, total: total + attend(me, h), zero, unroll=3)
    for k in send_order:
        source = seq_peer(k)

        def one_head(head, total, source=source):
            q_copy(me, source, head).wait_recv()
            return total + attend(source, head)

        vel_out[source] = lax.fori_loop(0, heads, one_head, zero, unroll=3)
        vel_copy(source, me).start()

    for k in range(1, n_seq):
        vel_copy(me, seq_peer(k)).wait_recv()
    velocity = vel_in[0]
    for k in range(1, n_seq):
        velocity = velocity + vel_in[k]
    latent = (noisy_ref[...] + step_size * velocity).astype(BF16)

    spread = dot(jnp.transpose(latent.astype(F32)).astype(BF16), spread_lanes)
    spread = jnp.where(in_place, spread, 0.0).astype(BF16)
    tiles_out[...] = (
        (dot(token_match, spread) + past_sent).astype(BF16).reshape(n_video, PACK, WIDE)
    )
    for k in range(1, n_video):
        tile_copy(video_peer(k), mv).start()
    tiles_in[mv] = tiles_out[mv]
    nl_ref[...] = latent

    shape = ((PAST + FRAMES) * rows, n_video * PACK)
    row = iota(shape, 0)
    item = row % rows
    frame = row // rows - PAST
    gather = one_hot(
        (iota(shape, 1) == item // CAP * PACK + frame * CAP + item % CAP) & (frame >= 0)
    )
    own[5 + heads].wait()
    for k in range(1, n_video):
        tile_copy(mv, video_peer(k)).wait_recv()
    frames = dot(gather, tiles_in[...].reshape(n_video * PACK, WIDE)).astype(BF16)
    taps = jnp.concatenate(
        [frames[dt * rows : (dt + FRAMES) * rows] for dt in range(3)], axis=1
    )

    def first_conv(cell, carry):
        hidden = dot(taps, toeplitz[cell].reshape(3 * WIDE, CH)).astype(BF16)
        wide = hidden.astype(F32)
        mean_square = jnp.mean(wide * wide, axis=-1, keepdims=True)
        unit = wide * lax.rsqrt(mean_square + 1e-06) * gain_ref[...]
        active = unit / (1.0 + jnp.exp(-unit))
        y, x = cell // TS, cell % TS
        field[y, x] = active.astype(BF16).reshape(FRAMES, rows, CH)
        acc[y, x] = wide[PAST * rows :].reshape(TPF, rows, CH)
        return carry

    lax.fori_loop(0, CELLS, first_conv, 0, unroll=4)

    for dy in range(3):
        for dx in range(3):
            y0, x0 = max(0, 1 - dy), max(0, 1 - dx)
            ny, nx = TS - abs(dy - 1), TS - abs(dx - 1)
            ys, xs = y0 + dy - 1, x0 + dx - 1
            lhs = jnp.concatenate(
                [
                    field[ys : ys + ny, xs : xs + nx, dt : dt + TPF].reshape(
                        ny * nx * TPF * rows, CH
                    )
                    for dt in range(3)
                ],
                axis=1,
            )
            product = dot(lhs, w2[:, dy * 3 + dx].reshape(3 * CH, CH))
            acc[y0 : y0 + ny, x0 : x0 + nx] += product.reshape(ny, nx, TPF, rows, CH)
    dec_ref[...] = acc[...].reshape(CELLS, TPF, rows, CH).astype(BF16)

    for k in range(1, n_seq):
        target = seq_peer(k)
        for part in range(4):
            kv_copy(target, me, part).wait_send()

        def sent_head(head, carry, target=target):
            q_copy(target, me, head).wait_send()
            return carry

        lax.fori_loop(0, heads, sent_head, 0)
        vel_copy(target, me).wait_send()
    for k in range(1, n_video):
        tile_copy(video_peer(k), mv).wait_send()


def on_device(
    n_seq,
    n_video,
    queries,
    kv_current,
    kv_history,
    noisy_latent,
    head_weight,
    timesteps,
    counts,
    past_latent,
    tile_lists,
    conv_in_weight,
    conv_weight,
    norm_gain,
):
    tokens = queries.shape[1]
    heads = QH // n_seq
    slots = kv_history.shape[1] + 1
    width = head_weight.shape[1]
    rows = n_video * CAP
    anywhere = pl.BlockSpec(memory_space=pl.ANY)
    vmem = pl.BlockSpec(memory_space=pltpu.VMEM)
    smem = pl.BlockSpec(memory_space=pltpu.SMEM)
    dma = pltpu.SemaphoreType.DMA
    next_latent, decoded = pl.pallas_call(
        functools.partial(step_kernel, n_seq, n_video),
        out_shape=(
            jax.ShapeDtypeStruct((width, tokens), BF16),
            jax.ShapeDtypeStruct((CELLS, TPF, rows, CH), BF16),
        ),
        in_specs=[
            anywhere,
            anywhere,
            anywhere,
            vmem,
            anywhere,
            smem,
            smem,
            vmem,
            smem,
            anywhere,
            anywhere,
            vmem,
        ],
        out_specs=(vmem, vmem),
        scratch_shapes=[
            pltpu.VMEM((n_seq, heads, tokens, HD), BF16),
            pltpu.VMEM((n_seq, slots, tokens, HD), BF16),
            pltpu.VMEM((n_seq, slots, tokens, HD), BF16),
            pltpu.VMEM((n_seq, slots, tokens, HD), BF16),
            pltpu.VMEM((n_seq, slots, tokens, 2 * HD), BF16),
            pltpu.VMEM((heads, width, HD), BF16),
            pltpu.VMEM((n_seq, width, tokens), F32),
            pltpu.VMEM((n_seq, width, tokens), F32),
            pltpu.VMEM((3, 9 * LC, CH), BF16),
            pltpu.VMEM((3, 9, CH, CH), BF16),
            pltpu.VMEM((CELLS, 3, WIDE, CH), BF16),
            pltpu.VMEM((n_video, PACK, WIDE), BF16),
            pltpu.VMEM((n_video, PACK, WIDE), BF16),
            pltpu.VMEM((TS, TS, FRAMES, rows, CH), BF16),
            pltpu.VMEM((TS, TS, TPF, rows, CH), F32),
            dma((n_seq, 4)),
            dma((n_seq, 4)),
            dma((n_seq, heads)),
            dma((n_seq, heads)),
            dma((n_seq,)),
            dma((n_seq,)),
            dma((n_video,)),
            dma((n_video,)),
            dma((6 + 2 * heads,)),
        ],
        compiler_params=pltpu.CompilerParams(
            collective_id=0, has_side_effects=True, vmem_limit_bytes=56 * 1024 * 1024
        ),
    )(
        queries[0],
        kv_current[0],
        kv_history[0],
        noisy_latent[0].T,
        head_weight.T,
        timesteps,
        counts,
        past_latent[0],
        tile_lists.reshape(-1),
        conv_in_weight.reshape(3, 9 * LC, CH),
        conv_weight.reshape(3, 9, CH, CH),
        norm_gain[None],
    )
    decoded = jnp.transpose(decoded, (2, 1, 0, 3)).reshape(1, rows, TPF * CELLS, CH)
    return next_latent.T[None], decoded


def solution(mesh):
    return jax.shard_map(
        functools.partial(on_device, mesh.shape["seq"], mesh.shape["video"]),
        mesh=mesh,
        in_specs=(
            P("video", "seq", None),
            P("video", "seq", None),
            P("video", None, "seq", None),
            P("video", "seq", None),
            P(),
            P("video"),
            P("video"),
            P("video", "seq", None),
            P("video", "seq", None),
            P(),
            P(),
            P(),
        ),
        out_specs=(P("video", "seq", None), P("video", "seq", None, None)),
        check_vma=False,
    )
```

```python
import functools
import math

import jax
import jax.numpy as jnp
from jax import lax
from jax.experimental import pallas as pl
from jax.experimental.pallas import tpu as pltpu
from jax.sharding import PartitionSpec as P

QH = 24
KVH = 4
HD = 128
LC = 16
CH = 256
TPF = 4
PAST = 2
TS = 4
CAP = 2
FRAMES = PAST + TPF
CELLS = TS * TS
WIDE = CELLS * LC
PACK = 16
MESH = pl.DeviceIdType.MESH
F32 = jnp.float32
BF16 = jnp.bfloat16


def noise_level(fraction):
    return 5.0 * fraction / (1.0 + 4.0 * fraction)


def iota(shape, axis):
    return lax.broadcasted_iota(jnp.int32, shape, axis)


def one_hot(condition):
    return jnp.where(condition, 1.0, 0.0).astype(BF16)


def dot(a, b):
    return jnp.dot(a, b, preferred_element_type=F32)


def step_kernel(
    n_seq,
    n_video,
    q_ref,
    kvc_ref,
    kvh_ref,
    noisy_ref,
    hw_ref,
    ts_ref,
    counts_ref,
    past_ref,
    lists_ref,
    win_ref,
    w2_ref,
    gain_ref,
    nl_ref,
    dec_ref,
    q_all,
    k_all,
    v_all,
    k_use,
    v_use,
    w_use,
    vel_out,
    vel_in,
    win,
    w2,
    toeplitz,
    tiles_out,
    tiles_in,
    field,
    acc,
    kv_send,
    kv_recv,
    q_send,
    q_recv,
    vel_send,
    vel_recv,
    tile_send,
    tile_recv,
    own_sem,
):
    me = lax.axis_index("seq")
    mv = lax.axis_index("video")
    heads = QH // n_seq
    group = QH // KVH
    slots = kvh_ref.shape[0] + 1
    tokens = q_ref.shape[0]
    tile_count = tokens // (TPF * 4)
    rows = n_video * CAP

    def seq_peer(k):
        if n_seq == 4:
            return (me + 1 - 2 * (me % 2), (me + 2) % 4, 3 - me)[k - 1]
        return (me + k) % n_seq

    def video_peer(k):
        return (mv + k) % n_video

    barrier = pltpu.get_barrier_semaphore()
    for k in range(1, n_seq):
        pl.semaphore_signal(barrier, inc=1, device_id=(seq_peer(k), mv), device_id_type=MESH)
    for k in range(1, n_video):
        pl.semaphore_signal(barrier, inc=1, device_id=(me, video_peer(k)), device_id_type=MESH)
    pl.semaphore_wait(barrier, n_seq + n_video - 2)

    def kv_parts(target, owner):
        column = pl.multiple_of((target * heads // group) * HD, HD)
        key_columns = pl.ds(column, HD)
        value_columns = pl.ds(pl.multiple_of(column + KVH * HD, HD), HD)
        return (
            (kvc_ref.at[:, key_columns], k_all.at[owner, 0]),
            (kvh_ref.at[:, :, key_columns], k_all.at[owner, pl.ds(1, slots - 1)]),
            (kvc_ref.at[:, value_columns], v_all.at[owner, 0]),
            (kvh_ref.at[:, :, value_columns], v_all.at[owner, pl.ds(1, slots - 1)]),
        )

    def kv_copy(target, owner, part):
        source, place = kv_parts(target, owner)[part]
        return pltpu.make_async_remote_copy(
            source,
            place,
            kv_send.at[target, part],
            kv_recv.at[owner, part],
            device_id=(target, mv),
            device_id_type=MESH,
        )

    def q_part(target, owner, head):
        column = pl.multiple_of((target * heads + head) * HD, HD)
        return q_ref.at[:, pl.ds(column, HD)], q_all.at[owner, head]

    def q_copy(target, owner, head):
        source, place = q_part(target, owner, head)
        return pltpu.make_async_remote_copy(
            source,
            place,
            q_send.at[target, head],
            q_recv.at[owner, head],
            device_id=(target, mv),
            device_id_type=MESH,
        )

    def vel_copy(target, owner):
        return pltpu.make_async_remote_copy(
            vel_out.at[target],
            vel_in.at[owner],
            vel_send.at[target],
            vel_recv.at[owner],
            device_id=(target, mv),
            device_id_type=MESH,
        )

    def tile_copy(target, owner):
        return pltpu.make_async_remote_copy(
            tiles_out.at[target],
            tiles_in.at[owner],
            tile_send.at[target],
            tile_recv.at[owner],
            device_id=(me, target),
            device_id_type=MESH,
        )

    send_order = range(n_seq - 1, 0, -1)
    for k in send_order:
        for part in range(4):
            kv_copy(seq_peer(k), me, part).start()

    def kv_sent(k):
        for part in range(4):
            kv_copy(seq_peer(k), me, part).wait_send()

    def send_heads(k, first, last):
        def one(head, carry):
            q_copy(seq_peer(k), me, head).start()
            return carry

        lax.fori_loop(first, last, one, 0)

    def heads_sent(k, first, last):
        def one(head, carry):
            q_copy(seq_peer(k), me, head).wait_send()
            return carry

        lax.fori_loop(first, last, one, 0)

    own = []
    for part, (source, place) in enumerate(kv_parts(me, me)):
        own.append(pltpu.make_async_copy(source, place, own_sem.at[part]))
    for head in range(heads):
        source, place = q_part(me, me, head)
        own.append(pltpu.make_async_copy(source, place, own_sem.at[4 + head]))
    own.append(pltpu.make_async_copy(win_ref, win, own_sem.at[4 + heads]))
    own.append(pltpu.make_async_copy(w2_ref, w2, own_sem.at[5 + heads]))
    for head in range(heads):
        columns = pl.ds(pl.multiple_of((me * heads + head) * HD, HD), HD)
        own.append(
            pltpu.make_async_copy(hw_ref.at[:, columns], w_use.at[head], own_sem.at[6 + heads + head])
        )
    for copy in own:
        copy.start()

    def clear(cell, carry):
        toeplitz[cell] = jnp.zeros(toeplitz.shape[1:], BF16)
        return carry

    lax.fori_loop(0, CELLS, clear, 0)
    own[4 + heads].wait()
    for y in range(TS):
        for x in range(TS):
            first = max(0, x - 1)
            count = min(TS, x + 2) - first
            for yy in range(max(0, y - 1), min(TS, y + 2)):
                to = (yy * TS + first) * LC
                start = ((yy - y + 1) * 3 + first - x + 1) * LC
                toeplitz[y * TS + x, :, to : to + count * LC, :] = win[:, start : start + count * LC, :]

    token_code = jnp.zeros((1, tokens), jnp.int32)
    past_code = jnp.zeros((1, PAST * tile_count), jnp.int32)
    token_tile = iota((1, tokens), 1) // (TPF * 4)
    past_tile = iota((1, PAST * tile_count), 1) % tile_count
    for t in range(tile_count):
        code = lists_ref[t] * CAP
        for t2 in range(t):
            code = code + jnp.where(lists_ref[t2] == lists_ref[t], 1, 0)
        token_code = jnp.where(token_tile == t, code, token_code)
        past_code = jnp.where(past_tile == t, code, past_code)
    out_rows = n_video * PACK

    def row_match(columns, code, frame):
        row = iota((out_rows, columns), 0)
        place = row % PACK
        row_code = (row // PACK) * CAP + place % CAP
        return one_hot((row_code == code) & (place // CAP == frame))

    token_match = row_match(tokens, token_code, iota((1, tokens), 1) // 4 % TPF + PAST)
    past_match = row_match(
        PAST * tile_count, past_code, iota((1, PAST * tile_count), 1) // tile_count
    )
    past_wide = past_ref[...].astype(F32)
    past_rows = jnp.concatenate(
        [past_wide[:, f * WIDE : (f + 1) * WIDE] for f in range(PAST)], axis=0
    ).astype(BF16)
    past_sent = dot(past_match, past_rows)

    width = hw_ref.shape[0]
    shape = (width, WIDE)
    lane = iota(shape, 1)
    cell = lane // LC
    spread_lanes = one_hot(iota(shape, 0) == (cell // TS % 2 * 2 + cell % 2) * LC + lane % LC)
    shape = (tokens, WIDE)
    cell = iota(shape, 1) // LC
    in_place = iota(shape, 0) % 4 == cell // TS // 2 * 2 + cell % TS // 2

    fraction = jnp.full((width, tokens), ts_ref[0], jnp.int32).astype(F32) / 1000.0
    step_size = noise_level(fraction - 0.25) - noise_level(fraction)

    held = jnp.full((tokens, HD), counts_ref[0], jnp.int32)

    def take_rows(source):
        key_rows = k_all[source, 0]
        k_use[source, 0] = key_rows
        v_use[source, 0, :, :HD] = v_all[source, 0]
        v_use[source, 0, :, HD:] = jnp.ones((tokens, HD), BF16)
        for slot in range(1, slots):
            valid = held >= slot
            k_use[source, slot] = jnp.where(
                valid, k_all[source, slot].astype(F32), key_rows.astype(F32)
            ).astype(BF16)
            v_use[source, slot, :, :HD] = jnp.where(
                valid, v_all[source, slot].astype(F32), 0.0
            ).astype(BF16)
            v_use[source, slot, :, HD:] = jnp.where(valid, 1.0, 0.0).astype(BF16)

    kv_sent(1)
    send_heads(1, 0, heads)
    for k in range(n_seq - 1, 1, -1):
        kv_sent(k)
        if k == n_seq - 1:
            send_heads(k, 0, heads)
    for part in range(4):
        own[part].wait()
    take_rows(me)
    for k in range(1, n_seq):
        source = seq_peer(k)
        for part in range(4):
            kv_copy(me, source, part).wait_recv()
        take_rows(source)

    scale = math.log2(math.e) / math.sqrt(HD)
    key_count = n_seq * slots * tokens

    def attend(source, head):
        keys = k_use[...].reshape(key_count, HD)
        scores = lax.dot_general(
            q_all[source, head], keys, (((1,), (1,)), ((), ())), preferred_element_type=F32
        )
        top = jnp.max(scores, axis=-1, keepdims=True)
        weights = jnp.exp2((scores - top) * scale).astype(BF16)
        mixed = dot(weights, v_use[...].reshape(key_count, 2 * HD))
        attended = (mixed[:, :HD] / mixed[:, HD:]).astype(BF16)
        return lax.dot_general(
            w_use[head], attended, (((1,), (1,)), ((), ())), preferred_element_type=F32
        )

    for head in range(heads):
        own[4 + head].wait()
        own[6 + heads + head].wait()
    zero = jnp.zeros((width, tokens), F32)
    vel_in[me] = lax.fori_loop(0, heads, lambda h, total: total + attend(me, h), zero, unroll=3)
    for k in (1, *range(n_seq - 1, 1, -1)):
        if k > 2:
            heads_sent(k, 0, heads)
            send_heads(k - 1, 0, heads)
        source = seq_peer(k)

        def one_head(head, total, source=source):
            q_copy(me, source, head).wait_recv()
            return total + attend(source, head)

        vel_out[source] = lax.fori_loop(0, heads, one_head, zero, unroll=3)
        vel_copy(source, me).start()

    for k in range(1, n_seq):
        vel_copy(me, seq_peer(k)).wait_recv()
    velocity = vel_in[0]
    for k in range(1, n_seq):
        velocity = velocity + vel_in[k]
    latent = (noisy_ref[...] + step_size * velocity).astype(BF16)

    spread = dot(jnp.transpose(latent.astype(F32)).astype(BF16), spread_lanes)
    spread = jnp.where(in_place, spread, 0.0).astype(BF16)
    tiles_out[...] = (
        (dot(token_match, spread) + past_sent).astype(BF16).reshape(n_video, PACK, WIDE)
    )
    for k in range(1, n_video):
        tile_copy(video_peer(k), mv).start()
    tiles_in[mv] = tiles_out[mv]
    nl_ref[...] = latent

    shape = ((PAST + FRAMES) * rows, n_video * PACK)
    row = iota(shape, 0)
    item = row % rows
    frame = row // rows - PAST
    gather = one_hot(
        (iota(shape, 1) == item // CAP * PACK + frame * CAP + item % CAP) & (frame >= 0)
    )
    own[5 + heads].wait()
    for k in range(1, n_video):
        tile_copy(mv, video_peer(k)).wait_recv()
    frames = dot(gather, tiles_in[...].reshape(n_video * PACK, WIDE)).astype(BF16)
    taps = jnp.concatenate(
        [frames[dt * rows : (dt + FRAMES) * rows] for dt in range(3)], axis=1
    )

    def first_conv(cell, carry):
        hidden = dot(taps, toeplitz[cell].reshape(3 * WIDE, CH)).astype(BF16)
        wide = hidden.astype(F32)
        mean_square = jnp.mean(wide * wide, axis=-1, keepdims=True)
        unit = wide * lax.rsqrt(mean_square + 1e-06) * gain_ref[...]
        active = unit / (1.0 + jnp.exp(-unit))
        y, x = cell // TS, cell % TS
        field[y, x] = active.astype(BF16).reshape(FRAMES, rows, CH)
        acc[y, x] = wide[PAST * rows :].reshape(TPF, rows, CH)
        return carry

    lax.fori_loop(0, CELLS, first_conv, 0, unroll=4)

    for dy in range(3):
        for dx in range(3):
            y0, x0 = max(0, 1 - dy), max(0, 1 - dx)
            ny, nx = TS - abs(dy - 1), TS - abs(dx - 1)
            ys, xs = y0 + dy - 1, x0 + dx - 1
            lhs = jnp.concatenate(
                [
                    field[ys : ys + ny, xs : xs + nx, dt : dt + TPF].reshape(
                        ny * nx * TPF * rows, CH
                    )
                    for dt in range(3)
                ],
                axis=1,
            )
            product = dot(lhs, w2[:, dy * 3 + dx].reshape(3 * CH, CH))
            acc[y0 : y0 + ny, x0 : x0 + nx] += product.reshape(ny, nx, TPF, rows, CH)
    dec_ref[...] = acc[...].reshape(CELLS, TPF, rows, CH).astype(BF16)

    for k in range(1, n_seq):
        if k == 1 or k == 2:
            heads_sent(k, 0, heads)
        vel_copy(seq_peer(k), me).wait_send()
    for k in range(1, n_video):
        tile_copy(video_peer(k), mv).wait_send()


def on_device(
    n_seq,
    n_video,
    queries,
    kv_current,
    kv_history,
    noisy_latent,
    head_weight,
    timesteps,
    counts,
    past_latent,
    tile_lists,
    conv_in_weight,
    conv_weight,
    norm_gain,
):
    tokens = queries.shape[1]
    heads = QH // n_seq
    slots = kv_history.shape[1] + 1
    width = head_weight.shape[1]
    rows = n_video * CAP
    anywhere = pl.BlockSpec(memory_space=pl.ANY)
    vmem = pl.BlockSpec(memory_space=pltpu.VMEM)
    smem = pl.BlockSpec(memory_space=pltpu.SMEM)
    dma = pltpu.SemaphoreType.DMA
    next_latent, decoded = pl.pallas_call(
        functools.partial(step_kernel, n_seq, n_video),
        out_shape=(
            jax.ShapeDtypeStruct((width, tokens), BF16),
            jax.ShapeDtypeStruct((CELLS, TPF, rows, CH), BF16),
        ),
        in_specs=[
            anywhere,
            anywhere,
            anywhere,
            vmem,
            anywhere,
            smem,
            smem,
            vmem,
            smem,
            anywhere,
            anywhere,
            vmem,
        ],
        out_specs=(vmem, vmem),
        scratch_shapes=[
            pltpu.VMEM((n_seq, heads, tokens, HD), BF16),
            pltpu.VMEM((n_seq, slots, tokens, HD), BF16),
            pltpu.VMEM((n_seq, slots, tokens, HD), BF16),
            pltpu.VMEM((n_seq, slots, tokens, HD), BF16),
            pltpu.VMEM((n_seq, slots, tokens, 2 * HD), BF16),
            pltpu.VMEM((heads, width, HD), BF16),
            pltpu.VMEM((n_seq, width, tokens), F32),
            pltpu.VMEM((n_seq, width, tokens), F32),
            pltpu.VMEM((3, 9 * LC, CH), BF16),
            pltpu.VMEM((3, 9, CH, CH), BF16),
            pltpu.VMEM((CELLS, 3, WIDE, CH), BF16),
            pltpu.VMEM((n_video, PACK, WIDE), BF16),
            pltpu.VMEM((n_video, PACK, WIDE), BF16),
            pltpu.VMEM((TS, TS, FRAMES, rows, CH), BF16),
            pltpu.VMEM((TS, TS, TPF, rows, CH), F32),
            dma((n_seq, 4)),
            dma((n_seq, 4)),
            dma((n_seq, heads)),
            dma((n_seq, heads)),
            dma((n_seq,)),
            dma((n_seq,)),
            dma((n_video,)),
            dma((n_video,)),
            dma((6 + 2 * heads,)),
        ],
        compiler_params=pltpu.CompilerParams(
            collective_id=0, has_side_effects=True, vmem_limit_bytes=56 * 1024 * 1024
        ),
    )(
        queries[0],
        kv_current[0],
        kv_history[0],
        noisy_latent[0].T,
        head_weight.T,
        timesteps,
        counts,
        past_latent[0],
        tile_lists.reshape(-1),
        conv_in_weight.reshape(3, 9 * LC, CH),
        conv_weight.reshape(3, 9, CH, CH),
        norm_gain[None],
    )
    decoded = jnp.transpose(decoded, (2, 1, 0, 3)).reshape(1, rows, TPF * CELLS, CH)
    return next_latent.T[None], decoded


def solution(mesh):
    return jax.shard_map(
        functools.partial(on_device, mesh.shape["seq"], mesh.shape["video"]),
        mesh=mesh,
        in_specs=(
            P("video", "seq", None),
            P("video", "seq", None),
            P("video", None, "seq", None),
            P("video", "seq", None),
            P(),
            P("video"),
            P("video"),
            P("video", "seq", None),
            P("video", "seq", None),
            P(),
            P(),
            P(),
        ),
        out_specs=(P("video", "seq", None), P("video", "seq", None, None)),
        check_vma=False,
    )
```
